32 devices in a mesh: beam: 2 (over x), chan: 8 (over z, y), tm: 2 (over core).
Axes of the slice: x: 2, y: 2, z: 4, core: 2. Of those that a mesh axis runs over, the one named last changes fastest.
Arguments:
- filterbank: bfloat16 [4096, 4096], P(('beam', 'chan'), 'tm'), parts along dimension 0, may hold values from -2500 to 2500
- local_delays: int32 [2048, 64], P('chan'), may hold values from 0 to 63
- lower_rows: int32 [3, 512], P(None, 'chan'), may hold values from 0 to 63
- upper_rows: int32 [3, 512], P(None, 'chan'), may hold values from 0 to 63
- level_shifts: int32 [3, 512], P(None, 'chan'), may hold values from 0 to 127, as said below
- box_widths: int32 [8], replicated, may hold values from 1 to 128, as said below
Outputs:
- snr: float32 [8, 1024, 4096], P(None, ('beam', 'chan'), 'tm'), parts along dimension 1
The draws below stay inside these ranges and needn't reach their ends.
There are 2 independent parts, one for each index of `beam`. The reference program is written for one: setup_inputs(seed, part) draws one part's arguments, and reference() takes and returns one part's arrays. A program takes and returns all parts, laid end to end along the dimension named above; an argument that names none is the same for every part. Nothing has to cross between parts.
Inputs may be any that keep to these rules, and one draw needn't show every extreme that they name: `level_shifts`: at level j every entry is below 64 * 2**j // 2, and that bound less one occurs at every level. `box_widths`: entry i lies in [2**i, 2**(i+1)) for i below 7; the last entry is 128.
All inputs are finite; a program needn't handle non-finite values.
Results may differ from the reference program's by a relative error of at most 0.0014.
Values may be sent and summed in bfloat16 or wider, within the bound.
No kernel may reach another device: no remote copies, remote signals or barrier semaphores. Data moves between devices by JAX's collectives and lax.ppermute only.
A program may use at most 64 MiB of HBM per device.

```python
import math
import jax
import jax.numpy as jnp
from jax import lax

CH_DEV = 256
K = 64
DLOC = 64
NW = 8
XLEV = 3
WMAX = 128
CH = 2048
DMS = 512
TT = 4096
N_CHAN = 8


def draw_filterbank(key, part):
    key_gain = jax.random.fold_in(key, 11)
    key_noise = jax.random.fold_in(key, 12)
    moments = jnp.arange(TT, dtype=jnp.float32) / TT
    gains = jnp.exp(jax.random.uniform(key_gain, (CH, 1), minval=0.0, maxval=math.log(10.0)))
    envelope = jnp.exp(math.log(10.0) * moments)[None, :]
    noise = jnp.clip(jax.random.normal(key_noise, (CH, TT)), -6.0, 6.0)
    values = gains * envelope * noise
    return values.astype(jnp.bfloat16)


def draw_local_delays(key, part):
    key_values = jax.random.fold_in(key, 21)
    key_place = jax.random.fold_in(key, 22)
    values = jax.random.randint(key_values, (CH * K,), 0, DLOC)
    place = jax.random.randint(key_place, (), 0, CH * K)
    values = values.at[place].set(DLOC - 1)
    return values.reshape(CH, K).astype(jnp.int32)


def draw_level_shifts(key, part):
    layers = []
    for level in range(XLEV):
        bound = DLOC * 2 ** level // 2
        key_values = jax.random.fold_in(key, 100 + level)
        key_place = jax.random.fold_in(key, 200 + level)
        values = jax.random.randint(key_values, (DMS,), 0, bound)
        place = jax.random.randint(key_place, (), 0, DMS)
        layers.append(values.at[place].set(bound - 1))
    return jnp.stack(layers).astype(jnp.int32)


def draw_box_widths(key, part):
    lowest = 2 ** jnp.arange(NW, dtype=jnp.int32)
    extra = jax.random.randint(jax.random.fold_in(key, 31), (NW,), 0, 2 ** 20) % lowest
    widths = lowest + extra
    widths = widths.at[NW - 1].set(WMAX)
    return widths.astype(jnp.int32)


def set_ends(result, rng, low, largest):
    extent = result.shape
    spot = [jax.random.randint(jax.random.fold_in(rng, axis), (), 0, extent[axis]) for axis in range(len(extent))]
    result = result.at[tuple(spot)].set(low)
    longest = extent.index(max(extent))
    spot[longest] = (spot[longest] + 1) % extent[longest]
    return result.at[tuple(spot)].set(largest)


def setup_inputs(seed: int = 0, part: int = 0) -> dict:
    seeds = jax.random.split(jax.random.key(seed), 7)
    part_splits = jax.random.split(jax.random.fold_in(seeds[6], part), 7)
    filterbank = draw_filterbank(jax.random.fold_in(jax.random.fold_in(seeds[6], part), 71), part)
    local_delays = draw_local_delays(jax.random.fold_in(seeds[6], 71), part)
    lower_rows = set_ends(jax.random.randint(seeds[2], (XLEV, DMS), 0, K), jax.random.fold_in(seeds[2], 1), 0, K - 1).astype(jnp.int32)
    upper_rows = set_ends(jax.random.randint(seeds[3], (XLEV, DMS), 0, K), jax.random.fold_in(seeds[3], 1), 0, K - 1).astype(jnp.int32)
    level_shifts = draw_level_shifts(jax.random.fold_in(seeds[6], 71), part)
    box_widths = draw_box_widths(jax.random.fold_in(seeds[6], 71), part)
    return dict(filterbank=filterbank, local_delays=local_delays, lower_rows=lower_rows, upper_rows=upper_rows, level_shifts=level_shifts, box_widths=box_widths)


def delay_rows(series, shift_by, reach_now):
    length = series.shape[1]
    padded = jnp.pad(series, ((0, 0), (reach_now, 0)))

    def take_one(single, amount):
        return lax.dynamic_slice_in_dim(single, reach_now - amount, length, 0)
    return jax.vmap(take_one)(padded, shift_by)

def reference(filterbank, local_delays, lower_rows, upper_rows, level_shifts, box_widths):
    samples = filterbank.shape[1]
    channel_rows = filterbank.astype(jnp.float32).reshape(N_CHAN, CH_DEV, samples).transpose(1, 0, 2)
    channel_delays = local_delays.reshape(N_CHAN, CH_DEV, K).transpose(1, 0, 2)

    def block_series(single, amounts):
        padded = jnp.pad(single, (DLOC, 0))

        def take_one(amount):
            return lax.dynamic_slice_in_dim(padded, DLOC - amount, samples, 0)
        return jax.vmap(take_one)(amounts)

    def add_channel(summed, chan_item):
        rows_now, delays_now = chan_item
        return (summed + jax.vmap(block_series)(rows_now, delays_now), None)
    state, _ = lax.scan(add_channel, jnp.zeros((N_CHAN, K, samples), jnp.float32), (channel_rows, channel_delays))
    blocks = jnp.arange(N_CHAN, dtype=jnp.int32)
    for level in range(XLEV):
        bit_value = 2 ** level
        reach_now = DLOC * bit_value // 2
        low_block = blocks - (blocks & bit_value)
        high_block = low_block + bit_value
        low_index = lower_rows[level].reshape(N_CHAN, K)
        high_index = upper_rows[level].reshape(N_CHAN, K)
        shifts_now = level_shifts[level].reshape(N_CHAN * K)
        picked_low = state[low_block[:, None], low_index]
        picked_high = state[high_block[:, None], high_index].reshape(N_CHAN * K, samples)
        state = picked_low + delay_rows(picked_high, shifts_now, reach_now).reshape(N_CHAN, K, samples)
    series = state.reshape(N_CHAN * K, samples)
    mean_square = lax.optimization_barrier(jnp.mean(series * series, axis=1))
    inverse_rms = lax.rsqrt(mean_square + 1e-05)
    running = jnp.cumsum(jnp.pad(series, ((0, 0), (WMAX, 0))), axis=1)
    later_sum = running[:, WMAX:]

    def one_width(box_width):
        earlier = lax.dynamic_slice_in_dim(running, WMAX - box_width, samples, 1)
        return (later_sum - earlier) * inverse_rms[:, None] / jnp.sqrt(box_width.astype(jnp.float32))
    return lax.map(one_width, box_widths)
```

```python
import functools

import jax
import jax.numpy as jnp
from jax import lax
from jax.experimental import pallas as pl
from jax.experimental.pallas import tpu as pltpu
from jax.sharding import PartitionSpec as P

DLOC = 64
TILE = 128
FINE = 8
FULL = 32700.0
TINY = 1e-30
VMEM_LIMIT = 48 * 2**20
BF16 = jnp.bfloat16
F32 = jnp.float32


def vmem():
    return pl.BlockSpec(memory_space=pltpu.VMEM)


def smem():
    return pl.BlockSpec(memory_space=pltpu.SMEM)


def lanes(shape):
    return lax.broadcasted_iota(jnp.int32, shape, len(shape) - 1)


def code_rows(count):
    return count + 16 * pl.cdiv(pl.cdiv(count, TILE), 16)


def diagonal(rows):
    return lax.broadcasted_iota(jnp.int32, (rows, TILE), 0) == lanes((rows, TILE))


def power_of_two(exponent):
    return jnp.exp2(exponent).astype(BF16).astype(F32)


def encode(state_ref, code_ref, exponents):
    count = state_ref.shape[0]
    exponents[...] = jnp.zeros_like(exponents)
    for group, first in enumerate(range(0, count, TILE)):
        size = min(TILE, count - first)
        values = state_ref[pl.ds(first, size), :]
        largest = jnp.max(jnp.abs(values), axis=1, keepdims=True)
        exponent = jnp.floor(jnp.log2(jnp.maximum(largest, TINY))) + 1.0
        scaled = values * (power_of_two(-exponent) * FULL)
        code_ref[pl.ds(first, size), :] = jnp.round(scaled).astype(jnp.int32).astype(jnp.int16)
        column = jnp.where(diagonal(size), exponent, 0.0)
        exponents[pl.ds(group, 1), :] = jnp.sum(column, axis=0, keepdims=True)
    code_ref[pl.ds(count, exponents.shape[0]), :] = exponents[...].astype(jnp.int32).astype(jnp.int16)


def decode(code_ref, state_ref, offset, count):
    units = code_ref[pl.ds(count, code_ref.shape[0] - count), :].astype(F32)
    units = jnp.exp2(units)
    ones = jnp.ones((TILE, TILE), BF16)
    for group, first in enumerate(range(0, count, TILE)):
        size = min(TILE, count - first)
        spread = jnp.where(diagonal(size), units[group : group + 1, :], 0.0).astype(BF16)
        unit = jnp.dot(spread, ones, preferred_element_type=F32) * (1.0 / FULL)
        state_ref[pl.ds(offset + first, size), :] = code_ref[pl.ds(first, size), :].astype(F32) * unit


def dedisperse_kernel(first, last, rim_tiles, rim, block, delays, state, code, onehot, exponents):
    channels, trials = delays.shape
    coarse = DLOC // FINE
    tiles = last - first
    by_row = delays[...].astype(BF16).T
    one, zero = jnp.ones((), BF16), jnp.zeros((), BF16)
    for high in range(coarse):
        for low in range(FINE):
            chosen = by_row == jnp.array(high * FINE + low, BF16)
            onehot[pl.ds(high * trials, trials), pl.ds(low * channels, channels)] = jnp.where(chosen, one, zero)
    lane_wide = lanes((channels, TILE)).astype(F32).astype(BF16)
    lane = lanes((trials, TILE))

    def samples_of(tile):
        if tile < 0:
            return rim[:, pl.ds((tile + rim_tiles) * TILE, TILE)]
        return block[:, pl.ds(tile * TILE, TILE)]

    def later(before, now, amount):
        if amount == 0:
            return now
        mixed = jnp.where(lane_wide >= jnp.array(TILE - amount, BF16), before, now)
        return pltpu.roll(mixed, amount, 1)

    before_product = None
    tile = first - 1
    while tile < last:
        width = min(2, last - tile)
        parts = [samples_of(max(tile - 1, first - 1))] + [samples_of(tile + i) for i in range(width)]
        stacked = jnp.concatenate(
            [
                jnp.concatenate([later(parts[i], parts[i + 1], low) for i in range(width)], axis=1)
                for low in range(FINE)
            ],
            axis=0,
        )
        product = jnp.dot(onehot[...], stacked, preferred_element_type=F32)
        for i in range(width):
            now_product = product[:, i * TILE : (i + 1) * TILE]
            if tile + i >= first:
                total = now_product[:trials]
                for high in range(1, coarse):
                    rows = slice(high * trials, (high + 1) * trials)
                    mixed = jnp.where(lane >= TILE - high * FINE, before_product[rows], now_product[rows])
                    total = total + pltpu.roll(mixed, high * FINE, 1)
                state[pl.ds(tile + i - first, trials, stride=tiles), :] = total
            before_product = now_product
        tile += width
    encode(state, code, exponents)


def dedisperse(rim, block, delays, first, last):
    channels, trials = delays.shape
    count = trials * (last - first)
    rows = code_rows(count)
    return pl.pallas_call(
        functools.partial(dedisperse_kernel, first, last, rim.shape[1] // TILE),
        out_shape=(
            jax.ShapeDtypeStruct((count, TILE), F32),
            jax.ShapeDtypeStruct((rows, TILE), jnp.int16),
        ),
        in_specs=[vmem(), vmem(), vmem()],
        out_specs=(vmem(), vmem()),
        scratch_shapes=[
            pltpu.VMEM((trials * DLOC // FINE, channels * FINE), BF16),
            pltpu.VMEM((rows - count, TILE), F32),
        ],
        compiler_params=pltpu.CompilerParams(vmem_limit_bytes=VMEM_LIMIT),
        cost_estimate=pl.CostEstimate(
            flops=2 * count * TILE * DLOC * channels, bytes_accessed=4 * count * TILE, transcendentals=0
        ),
        name="dedisperse",
    )(rim, block, delays)


def merge_kernel(level, drop, front, side, lower, upper, shifts, own, partner, state, result, both, exponents):
    trials = lower.shape[1]
    count = own.shape[0]
    tiles = count // trials
    kept = tiles - drop
    second = 2 * front + count
    both[pl.ds(0, front), :] = jnp.zeros((front, TILE), F32)
    both[pl.ds(front + count, front), :] = jnp.zeros((front, TILE), F32)
    both[pl.ds(front, count), :] = own[...]
    decode(partner, both, second, count)
    on_upper = side[level] == 1
    low_base = jnp.where(on_upper, second, front) + drop
    high_base = jnp.where(on_upper, front, second) + drop
    for row in range(trials):
        low_at = low_base + lower[level, row] * tiles
        shift = shifts[level, row]
        turn = shift & (TILE - 1)
        high_at = high_base + upper[level, row] * tiles - (shift >> 7)
        for start in range(0, kept, 8):
            size = min(8, kept - start)
            now = both[pl.ds(high_at + start, size), :]
            before = both[pl.ds(high_at + start - 1, size), :]
            mixed = jnp.where(lanes((size, TILE)) >= TILE - turn, before, now)
            merged = both[pl.ds(low_at + start, size), :] + pltpu.roll(mixed, turn, 1)
            state[pl.ds(row * kept + start, size), :] = merged
    if result.dtype == jnp.int16:
        encode(state, result, exponents)
    else:
        halo = kept - exponents.shape[0]
        total = jnp.zeros((trials, TILE), F32)
        for tile in range(halo, kept):
            values = state[pl.ds(tile, trials, stride=kept), :]
            total = total + values * values
        result[...] = jnp.broadcast_to(jnp.sum(total, axis=1, keepdims=True), total.shape)


def merge(tables, own, partner, level, drop, reach, last_tiles):
    trials = tables[1].shape[1]
    count = own.shape[0]
    kept = trials * (count // trials - drop)
    rows = code_rows(kept)
    front = 8 * pl.cdiv((reach - 1) // TILE + 1, 8)
    if last_tiles:
        result, spare = jax.ShapeDtypeStruct((trials, TILE), F32), last_tiles
    else:
        result, spare = jax.ShapeDtypeStruct((rows, TILE), jnp.int16), rows - kept
    return pl.pallas_call(
        functools.partial(merge_kernel, level, drop, front),
        out_shape=(jax.ShapeDtypeStruct((kept, TILE), F32), result),
        in_specs=[smem()] * 4 + [vmem(), vmem()],
        out_specs=(vmem(), vmem()),
        scratch_shapes=[
            pltpu.VMEM((2 * front + 2 * count, TILE), F32),
            pltpu.VMEM((spare, TILE), F32),
        ],
        compiler_params=pltpu.CompilerParams(vmem_limit_bytes=VMEM_LIMIT),
        name="merge_rows",
    )(*tables, own, partner)


def boxcar_kernel(times, group, widths, state, mine, others, snr, split):
    trials = mine.shape[0]
    tiles = state.shape[0] // trials
    halo = tiles - snr.shape[2] // TILE
    step = pl.program_id(0)

    @pl.when(step == 0)
    def _():
        before = None
        for tile in range(halo - 1, tiles):
            values = state[pl.ds(tile, trials, stride=tiles), :]
            coarse = values.astype(BF16)
            fine = (values - coarse.astype(F32)).astype(BF16)
            now = (coarse, fine)
            if before is not None:
                at = pl.ds((tile - halo) * trials, trials)
                for i, part in enumerate((before[0], now[0], before[1], now[1])):
                    split[at, pl.ds(i * TILE, TILE)] = part
            before = now

    from_start = lax.broadcasted_iota(jnp.int32, (2 * TILE, TILE), 0) - TILE
    back = lanes((2 * TILE, TILE)) - from_start
    inverse_rms = lax.rsqrt((mine[...] + others[...]) / times + 1e-05)
    masks, scales = [], []
    for i in range(group):
        width = widths[step * group + i]
        masks.append(jnp.where((back >= 0) & (back < width), 1.0, 0.0).astype(BF16))
        scales.append(inverse_rms / jnp.sqrt(jnp.full(inverse_rms.shape, width, jnp.int32).astype(F32)))
    mask = jnp.concatenate(masks, axis=1)
    boxes = jnp.dot(split[...], jnp.concatenate([mask, mask], axis=0), preferred_element_type=F32)
    for tile in range(tiles - halo):
        for i in range(group):
            values = boxes[tile * trials : (tile + 1) * trials, i * TILE : (i + 1) * TILE]
            snr[i, :, pl.ds(tile * TILE, TILE)] = values * scales[i]


def boxcar(widths, state, mine, others, samples, times):
    trials = mine.shape[0]
    count = widths.shape[0]
    group = 2
    whole = lambda shape: pl.BlockSpec(shape, lambda i: (0, 0))
    return pl.pallas_call(
        functools.partial(boxcar_kernel, times, group),
        grid=(count // group,),
        out_shape=jax.ShapeDtypeStruct((count, trials, samples), F32),
        in_specs=[smem(), whole(state.shape), whole(mine.shape), whole(others.shape)],
        out_specs=pl.BlockSpec((group, trials, samples), lambda i: (i, 0, 0)),
        scratch_shapes=[pltpu.VMEM((trials * samples // TILE, 4 * TILE), BF16)],
        compiler_params=pltpu.CompilerParams(vmem_limit_bytes=VMEM_LIMIT),
        name="boxcar",
    )(widths, state, mine, others)


def tail_of_previous(block, length, axis):
    samples = block.shape[1]
    devices = lax.axis_size(axis)
    parts = []
    for hop in range(1, pl.cdiv(length, samples) + 1):
        take = min(samples, length - (hop - 1) * samples)
        part = block[:, samples - take :]
        if hop < devices:
            part = lax.ppermute(part, axis, [(i - hop, i) for i in range(hop, devices)])
        else:
            part = jnp.zeros_like(part)
        parts.insert(0, part)
    return jnp.concatenate(parts, axis=1) if len(parts) > 1 else parts[0]


def sum_of_others(value, axis):
    devices = lax.axis_size(axis)
    total = None
    for hop in range(1, devices):
        part = lax.ppermute(value, axis, [(i, (i + hop) % devices) for i in range(devices)])
        total = part if total is None else total + part
    return jnp.zeros_like(value) if total is None else total


def local(filterbank, local_delays, lower_rows, upper_rows, level_shifts, box_widths):
    samples = filterbank.shape[1]
    devices = lax.axis_size("chan")
    levels = devices.bit_length() - 1
    widest = 2 ** (box_widths.shape[0] - 1)
    reaches = [DLOC * 2**level // 2 for level in range(levels)]
    needs = [widest - 1]
    for reach in reversed(reaches):
        needs.insert(0, needs[0] + reach - 1)
    halos = [pl.cdiv(need, TILE) for need in needs]
    rim_tiles = max(pl.cdiv(needs[0] + DLOC - 1, TILE), halos[0] + 1)
    rim = tail_of_previous(filterbank, rim_tiles * TILE, "tm")
    here = lax.axis_index("chan")
    side = jnp.stack([here >> level & 1 for level in range(levels)])
    tables = (side, lower_rows, upper_rows, level_shifts)
    tiles = samples // TILE
    state, code = dedisperse(rim, filterbank, local_delays, -halos[0], tiles)
    for level in range(levels):
        partner = lax.ppermute(code, "chan", [(i, i ^ 1 << level) for i in range(devices)])
        drop = halos[level] - halos[level + 1]
        last_tiles = tiles if level == levels - 1 else 0
        state, code = merge(tables, state, partner, level, drop, reaches[level], last_tiles)
    others = sum_of_others(code, "tm")
    return boxcar(box_widths, state, code, others, samples, samples * lax.axis_size("tm"))


def solution(mesh):
    placed = (
        P(("beam", "chan"), "tm"),
        P("chan", None),
        P(None, "chan"),
        P(None, "chan"),
        P(None, "chan"),
        P(),
    )
    return jax.shard_map(
        local,
        mesh=mesh,
        in_specs=placed,
        out_specs=P(None, ("beam", "chan"), "tm"),
        check_vma=False,
    )
```

```python
import functools

import jax
import jax.numpy as jnp
from jax import lax
from jax.experimental import pallas as pl
from jax.experimental.pallas import tpu as pltpu
from jax.sharding import PartitionSpec as P

DLOC = 64
TILE = 128
FINE = 8
CHUNKS = 2
FULL = 32700.0
TINY = 1e-30
UPPER = 1 << 30
LAST = 1 << 29
VMEM_LIMIT = 48 * 2**20
BF16 = jnp.bfloat16
F32 = jnp.float32


def vmem():
    return pl.BlockSpec(memory_space=pltpu.VMEM)


def smem():
    return pl.BlockSpec(memory_space=pltpu.SMEM)


def lanes(shape):
    return lax.broadcasted_iota(jnp.int32, shape, len(shape) - 1)


def code_rows(count):
    return count + 16 * pl.cdiv(pl.cdiv(count, TILE), 16)


def diagonal(rows):
    return lax.broadcasted_iota(jnp.int32, (rows, TILE), 0) == lanes((rows, TILE))


def power_of_two(exponent):
    return jnp.exp2(exponent).astype(BF16).astype(F32)


def encode(state_ref, code_ref, exponents):
    count = state_ref.shape[0]
    exponents[...] = jnp.zeros_like(exponents)
    for group, first in enumerate(range(0, count, TILE)):
        size = min(TILE, count - first)
        values = state_ref[pl.ds(first, size), :]
        largest = jnp.max(jnp.abs(values), axis=1, keepdims=True)
        exponent = jnp.floor(jnp.log2(jnp.maximum(largest, TINY))) + 1.0
        scaled = values * (power_of_two(-exponent) * FULL)
        code_ref[pl.ds(first, size), :] = jnp.round(scaled).astype(jnp.int32).astype(jnp.int16)
        column = jnp.where(diagonal(size), exponent, 0.0)
        exponents[pl.ds(group, 1), :] = jnp.sum(column, axis=0, keepdims=True)
    code_ref[pl.ds(count, exponents.shape[0]), :] = exponents[...].astype(jnp.int32).astype(jnp.int16)


def decode(code_ref, state_ref, offset, count):
    units = code_ref[pl.ds(count, code_ref.shape[0] - count), :].astype(F32)
    units = jnp.exp2(units)
    ones = jnp.ones((TILE, TILE), BF16)
    for group, first in enumerate(range(0, count, TILE)):
        size = min(TILE, count - first)
        spread = jnp.where(diagonal(size), units[group : group + 1, :], 0.0).astype(BF16)
        unit = jnp.dot(spread, ones, preferred_element_type=F32) * (1.0 / FULL)
        state_ref[pl.ds(offset + first, size), :] = code_ref[pl.ds(first, size), :].astype(F32) * unit


def load_kernel(*refs):
    *refs, sems = refs
    half = (len(refs) - 1) // 2
    sources, (edge, *targets) = refs[:half], refs[half:]
    start = sources[0].shape[1] - edge.shape[1]
    copies = [pltpu.make_async_copy(sources[0].at[:, pl.ds(start, edge.shape[1])], edge, sems.at[half])]
    copies += [pltpu.make_async_copy(source, target, sems.at[i]) for i, (source, target) in enumerate(zip(sources, targets))]
    for copy in copies:
        copy.start()
    for copy in copies:
        copy.wait()


def load(length, *arrays):
    edge = jax.ShapeDtypeStruct((arrays[0].shape[0], length), arrays[0].dtype)
    return pl.pallas_call(
        load_kernel,
        out_shape=[edge] + [jax.ShapeDtypeStruct(array.shape, array.dtype) for array in arrays],
        in_specs=[pl.BlockSpec(memory_space=pltpu.HBM)] * len(arrays),
        out_specs=[vmem()] * (len(arrays) + 1),
        scratch_shapes=[pltpu.SemaphoreType.DMA((len(arrays) + 1,))],
        compiler_params=pltpu.CompilerParams(vmem_limit_bytes=VMEM_LIMIT),
        name="load",
    )(*[pltpu.with_memory_space_constraint(array, pltpu.HBM) for array in arrays])


def prepare_kernel(flags, delays, lower, upper, shifts, widths, onehot, table, masks, roots):
    trials, channels = delays.shape
    bits = (trials - 1).bit_length()
    for level in range(table.shape[0]):
        row = pl.ds(level, 1)
        table[row, :] = lower[row, :] | upper[row, :] << bits | shifts[row, :] << 2 * bits | flags[row, :]
    by_row = delays[...].astype(F32).astype(BF16)
    one, zero = jnp.ones((), BF16), jnp.zeros((), BF16)
    for high in range(DLOC // FINE):
        for low in range(FINE):
            chosen = by_row == jnp.array(high * FINE + low, BF16)
            onehot[pl.ds(high * trials, trials), pl.ds(low * channels, channels)] = jnp.where(chosen, one, zero)
    from_start = lax.broadcasted_iota(jnp.int32, (2 * TILE, TILE), 0) - TILE
    back = lanes((2 * TILE, TILE)) - from_start
    all_widths = widths[...]
    for i in range(roots.shape[0]):
        width = all_widths[0, i]
        masks[:, pl.ds(i * TILE, TILE)] = jnp.where((back >= 0) & (back < width), 1.0, 0.0).astype(BF16)
        roots[pl.ds(i, 1), :] = 1.0 / jnp.sqrt(jnp.full((1, TILE), width, jnp.int32).astype(F32))


def prepare(flags, delays, lower, upper, shifts, widths):
    trials, channels = delays.shape
    count = widths.shape[1]
    operands = (flags, delays, lower, upper, shifts, widths)
    return pl.pallas_call(
        prepare_kernel,
        out_shape=(
            jax.ShapeDtypeStruct((trials * DLOC // FINE, channels * FINE), BF16),
            jax.ShapeDtypeStruct(lower.shape, jnp.int32),
            jax.ShapeDtypeStruct((2 * TILE, count * TILE), BF16),
            jax.ShapeDtypeStruct((count, TILE), F32),
        ),
        in_specs=[vmem() for _ in operands],
        out_specs=(vmem(),) * 4,
        compiler_params=pltpu.CompilerParams(vmem_limit_bytes=VMEM_LIMIT),
        name="prepare",
    )(*operands)


def dedisperse_kernel(first, last, rim_tiles, *refs):
    *rims, block, onehot, state, code, exponents = refs
    channels = block.shape[0]
    coarse = DLOC // FINE
    trials = onehot.shape[0] // coarse
    tiles = last - first
    lane_wide = lanes((channels, TILE)).astype(F32).astype(BF16)
    lane = lanes((trials, TILE))

    def samples_of(tile):
        if tile < 0:
            return rims[0][:, pl.ds((tile + rim_tiles) * TILE, TILE)]
        return block[:, pl.ds(tile * TILE, TILE)]

    def later(before, now, amount):
        if amount == 0:
            return now
        mixed = jnp.where(lane_wide >= jnp.array(TILE - amount, BF16), before, now)
        return pltpu.roll(mixed, amount, 1)

    before_product = None
    tile = first - 1
    while tile < last:
        width = min(2, last - tile)
        parts = [samples_of(max(tile - 1, first - 1))] + [samples_of(tile + i) for i in range(width)]
        stacked = jnp.concatenate(
            [
                jnp.concatenate([later(parts[i], parts[i + 1], low) for i in range(width)], axis=1)
                for low in range(FINE)
            ],
            axis=0,
        )
        product = jnp.dot(onehot[...], stacked, preferred_element_type=F32)
        for i in range(width):
            now_product = product[:, i * TILE : (i + 1) * TILE]
            if tile + i >= first:
                total = now_product[:trials]
                for high in range(1, coarse):
                    rows = slice(high * trials, (high + 1) * trials)
                    mixed = jnp.where(lane >= TILE - high * FINE, before_product[rows], now_product[rows])
                    total = total + pltpu.roll(mixed, high * FINE, 1)
                state[pl.ds(tile + i - first, trials, stride=tiles), :] = total
            before_product = now_product
        tile += width
    encode(state, code, exponents)


def dedisperse(rim, block, onehot, first, last):
    channels = block.shape[0]
    trials = onehot.shape[0] // (DLOC // FINE)
    count = trials * (last - first)
    rows = code_rows(count)
    operands = ([rim] if first < 1 else []) + [block, onehot]
    return pl.pallas_call(
        functools.partial(dedisperse_kernel, first, last, rim.shape[1] // TILE),
        out_shape=(
            jax.ShapeDtypeStruct((count, TILE), F32),
            jax.ShapeDtypeStruct((rows, TILE), jnp.int16),
        ),
        in_specs=[vmem() for _ in operands],
        out_specs=(vmem(), vmem()),
        scratch_shapes=[pltpu.VMEM((rows - count, TILE), F32)],
        compiler_params=pltpu.CompilerParams(vmem_limit_bytes=VMEM_LIMIT),
        cost_estimate=pl.CostEstimate(
            flops=2 * count * TILE * DLOC * channels, bytes_accessed=4 * count * TILE, transcendentals=0
        ),
        name="dedisperse",
    )(*operands)


def merge_kernel(plan, *refs):
    level, drop, front, history, has_before, has_tail, is_last = plan
    refs = list(refs)
    table, own, partner = refs[:3]
    del refs[:3]
    before_tail = refs.pop(0) if has_before else None
    before_sum = refs.pop(0) if has_before and is_last else None
    state, result = refs[:2]
    del refs[:2]
    tail = refs.pop(0) if has_tail else None
    both, flat, exponents = refs
    trials = table.shape[1]
    bits = (trials - 1).bit_length()
    count = own.shape[0]
    tiles = count // trials
    kept = tiles - drop
    left = history if has_before else 0
    stride = left + tiles
    second = 2 * front + trials * stride
    both[pl.ds(0, front), :] = jnp.zeros((front, TILE), F32)
    both[pl.ds(second - front, front), :] = jnp.zeros((front, TILE), F32)
    if left:
        decode(partner, flat, 0, count)
        for base, now, at in ((front, own, 0), (second, flat, trials * left)):
            for row in range(trials):
                both[pl.ds(base + row * stride + left, tiles), :] = now[pl.ds(row * tiles, tiles), :]
            for tile in range(left):
                both[pl.ds(base + tile, trials, stride=stride), :] = before_tail[pl.ds(at + tile, trials, stride=left), :]
    else:
        both[pl.ds(front, count), :] = own[...]
        decode(partner, both, second, count)
    if has_tail:
        for base, at in ((front, 0), (second, trials * history)):
            for tile in range(history):
                values = both[pl.ds(base + stride - history + tile, trials, stride=stride), :]
                tail[pl.ds(at + tile, trials, stride=history), :] = values
    entries = table[pl.ds(level, 1), :]
    on_upper = entries[0, 0] & UPPER != 0
    low_base = jnp.where(on_upper, second, front) + left + drop
    high_base = jnp.where(on_upper, front, second) + left + drop
    for row in range(trials):
        entry = entries[0, row] & LAST - 1
        low_at = low_base + (entry & (1 << bits) - 1) * stride
        shift = entry >> 2 * bits
        turn = shift & (TILE - 1)
        high_at = high_base + (entry >> bits & (1 << bits) - 1) * stride - (shift >> 7)
        for start in range(0, kept, 8):
            size = min(8, kept - start)
            now = both[pl.ds(high_at + start, size), :]
            before = both[pl.ds(high_at + start - 1, size), :]
            mixed = jnp.where(lanes((size, TILE)) >= TILE - turn, before, now)
            merged = both[pl.ds(low_at + start, size), :] + pltpu.roll(mixed, turn, 1)
            state[pl.ds(row * kept + start, size), :] = merged
    if is_last:
        total = jnp.zeros((trials, TILE), F32)
        for tile in range(kept):
            values = state[pl.ds(tile, trials, stride=kept), :]
            total = total + values * values
        total = jnp.broadcast_to(jnp.sum(total, axis=1, keepdims=True), total.shape)
        result[pl.ds(0, trials), :] = total + before_sum[pl.ds(0, trials), :] if has_before else total
        result[pl.ds(trials, trials), :] = jnp.where(entries[0, 0] & LAST != 0, 0.0, values)
    else:
        encode(state, result, exponents)


def merge(table, own, partner, before, level, drop, history, has_tail, is_last):
    trials = table.shape[1]
    count = own.shape[0]
    tiles = count // trials
    kept = trials * (tiles - drop)
    rows = code_rows(kept)
    front = 8 * pl.cdiv(history, 8)
    has_before = before is not None
    plan = (level, drop, front, history, has_before, has_tail, is_last)
    operands = [table, own, partner]
    if has_before:
        operands += [before[0], before[1]] if is_last else [before[0]]
    shapes = [jax.ShapeDtypeStruct((kept, TILE), F32)]
    if is_last:
        shapes.append(jax.ShapeDtypeStruct((2 * trials, TILE), F32))
    else:
        shapes.append(jax.ShapeDtypeStruct((rows, TILE), jnp.int16))
    if has_tail:
        shapes.append(jax.ShapeDtypeStruct((2 * trials * history, TILE), F32))
    stride = tiles + (history if has_before else 0)
    state, result, *tail = pl.pallas_call(
        functools.partial(merge_kernel, plan),
        out_shape=shapes,
        in_specs=[vmem() for _ in operands],
        out_specs=[vmem() for _ in shapes],
        scratch_shapes=[
            pltpu.VMEM((2 * front + 2 * trials * stride, TILE), F32),
            pltpu.VMEM((count if has_before else 8, TILE), F32),
            pltpu.VMEM((rows - kept, TILE), F32),
        ],
        compiler_params=pltpu.CompilerParams(vmem_limit_bytes=VMEM_LIMIT),
        cost_estimate=pl.CostEstimate(flops=20 * kept * TILE, bytes_accessed=16 * kept * TILE, transcendentals=0),
        name="merge_rows",
    )(*operands)
    return state, result, (tail[0] if has_tail else None)


def two_terms(values):
    coarse = values.astype(BF16)
    return coarse, (values - coarse.astype(F32)).astype(BF16)


def boxcar_kernel(masks, state, *refs):
    *befores, boxes, split = refs
    count, trials, samples = boxes.shape
    tiles = samples // TILE
    if befores:
        length = befores[0].shape[0] // trials
        before = two_terms(befores[0][pl.ds(length - 1, trials, stride=length), :])
    else:
        before = two_terms(jnp.zeros((trials, TILE), F32))
    for tile in range(tiles):
        now = two_terms(state[pl.ds(tile, trials, stride=tiles), :])
        for i, part in enumerate((before[0], now[0], before[1], now[1])):
            split[pl.ds(tile * trials, trials), pl.ds(i * TILE, TILE)] = part
        before = now
    for first in range(0, count, 2):
        mask = masks[:, pl.ds(first * TILE, 2 * TILE)]
        sums = jnp.dot(split[...], jnp.concatenate([mask, mask], axis=0), preferred_element_type=F32)
        for tile in range(tiles):
            for i in range(2):
                values = sums[tile * trials : (tile + 1) * trials, i * TILE : (i + 1) * TILE]
                boxes[first + i, :, pl.ds(tile * TILE, TILE)] = values


def boxcar(masks, state, before, trials):
    count = masks.shape[1] // TILE
    tiles = state.shape[0] // trials
    operands = [masks, state] + ([] if before is None else [before])
    return pl.pallas_call(
        boxcar_kernel,
        out_shape=jax.ShapeDtypeStruct((count, trials, tiles * TILE), F32),
        in_specs=[vmem() for _ in operands],
        out_specs=vmem(),
        scratch_shapes=[pltpu.VMEM((trials * tiles, 4 * TILE), BF16)],
        compiler_params=pltpu.CompilerParams(vmem_limit_bytes=VMEM_LIMIT),
        cost_estimate=pl.CostEstimate(
            flops=8 * count * trials * tiles * TILE * TILE, bytes_accessed=4 * count * trials * tiles * TILE, transcendentals=0
        ),
        name="boxcar",
    )(*operands)


def scale_kernel(times, masks, roots, mine, other, *refs):
    *parts, snr, scaled, sems = refs
    count, trials = parts[0].shape[:2]
    inverse_rms = lax.rsqrt((mine[pl.ds(0, trials), :] + other[pl.ds(0, trials), :]) / times + 1e-05)
    rim = jnp.concatenate(two_terms(other[pl.ds(trials, trials), :]), axis=1)
    copies = []
    for i in range(count):
        scale = inverse_rms * roots[pl.ds(i, 1), :]
        mask = masks[pl.ds(0, TILE), pl.ds(i * TILE, TILE)]
        into_first = jnp.dot(rim, jnp.concatenate([mask, mask], axis=0), preferred_element_type=F32)
        start = 0
        for part in parts:
            for at in range(0, part.shape[2], TILE):
                values = part[i, :, pl.ds(at, TILE)]
                if start + at == 0:
                    values = values + into_first
                scaled[i, :, pl.ds(start + at, TILE)] = values * scale
            start += part.shape[2]
        copies.append(pltpu.make_async_copy(scaled.at[i], snr.at[i], sems.at[i]))
        copies[-1].start()
    for copy in copies:
        copy.wait()


def scaled(masks, roots, mine, other, parts, times):
    count, trials = parts[0].shape[:2]
    samples = sum(part.shape[2] for part in parts)
    operands = [masks, roots, mine, other, *parts]
    return pl.pallas_call(
        functools.partial(scale_kernel, times),
        out_shape=jax.ShapeDtypeStruct((count, trials, samples), F32),
        in_specs=[vmem() for _ in operands],
        out_specs=pl.BlockSpec(memory_space=pltpu.HBM),
        scratch_shapes=[pltpu.VMEM((count, trials, samples), F32), pltpu.SemaphoreType.DMA((count,))],
        compiler_params=pltpu.CompilerParams(vmem_limit_bytes=VMEM_LIMIT),
        name="scale",
    )(*operands)


def tail_of_previous(block, edge, length, axis):
    samples = block.shape[1]
    devices = lax.axis_size(axis)
    parts = []
    for hop in range(1, pl.cdiv(length, samples) + 1):
        take = min(samples, length - (hop - 1) * samples)
        if hop < devices:
            part = edge if hop == 1 else block[:, samples - take :]
            part = lax.ppermute(part, axis, [(i - hop, i) for i in range(hop, devices)])
        else:
            part = jnp.zeros((block.shape[0], take), block.dtype)
        parts.insert(0, part)
    return jnp.concatenate(parts, axis=1) if len(parts) > 1 else parts[0]


def local(filterbank, local_delays, lower_rows, upper_rows, level_shifts, box_widths):
    samples = filterbank.shape[1]
    trials = local_delays.shape[1]
    devices = lax.axis_size("chan")
    levels = devices.bit_length() - 1
    reaches = [DLOC * 2**level // 2 for level in range(levels)]
    needs = [0]
    for reach in reversed(reaches):
        needs.insert(0, needs[0] + reach - 1)
    halos = [pl.cdiv(need, TILE) for need in needs]
    rim_tiles = max(pl.cdiv(needs[0] + DLOC - 1, TILE), halos[0] + 1)
    edge, block, *tables = load(
        min(samples, rim_tiles * TILE),
        filterbank,
        local_delays.T,
        lower_rows,
        upper_rows,
        level_shifts,
        box_widths.reshape(1, -1),
    )
    rim = tail_of_previous(block, edge, rim_tiles * TILE, "tm")
    here = lax.axis_index("chan")
    blocks = lax.axis_size("tm")
    flag = jnp.where(lax.axis_index("tm") == blocks - 1, LAST, 0)
    flags = jnp.stack([flag + (here >> level & 1) * UPPER for level in range(levels)])
    flags = jnp.broadcast_to(flags[:, None], (levels, trials))
    onehot, table, masks, roots = prepare(flags, *tables)
    tiles = samples // TILE
    histories = [(reach - 1) // TILE + 1 for reach in reaches]
    chunks = max(1, min(CHUNKS, tiles // max(histories)))
    ends = [max(tiles * (i + 1) // chunks - (halos[0] // 2 if i + 1 < chunks else 0), max(histories)) for i in range(chunks)]
    starts = [-halos[0]] + ends[:-1]
    states, codes = [], []
    for k in range(chunks):
        state, code = dedisperse(rim, block, onehot, starts[k], ends[k])
        code, onehot = lax.optimization_barrier((code, onehot))
        states.append(state)
        codes.append(code)
    boxes = []
    for level in range(levels):
        before = None
        is_last = level == levels - 1
        for k in range(chunks):
            partner = lax.ppermute(codes[k], "chan", [(i, i ^ 1 << level) for i in range(devices)])
            if is_last and k:
                *boxes, partner = lax.optimization_barrier((*boxes, partner))
            drop = halos[level] - halos[level + 1] if k == 0 else 0
            states[k], codes[k], tail = merge(
                table, states[k], partner, before, level, drop, histories[level], k + 1 < chunks, is_last
            )
            before = (tail, codes[k])
            if is_last:
                boxes.append(boxcar(masks, states[k], states[k - 1] if k else None, trials))
    mine = codes[-1]
    other = jnp.zeros_like(mine)
    for hop in range(1, blocks):
        part = lax.ppermute(mine, "tm", [(i, (i + hop) % blocks) for i in range(blocks)])
        other = part if hop == 1 else other.at[:trials].add(part[:trials])
    return scaled(masks, roots, mine, other, boxes, samples * blocks)


def solution(mesh):
    placed = (
        P(("beam", "chan"), "tm"),
        P("chan", None),
        P(None, "chan"),
        P(None, "chan"),
        P(None, "chan"),
        P(),
    )
    return jax.shard_map(
        local,
        mesh=mesh,
        in_specs=placed,
        out_specs=P(None, ("beam", "chan"), "tm"),
        check_vma=False,
    )
```
